32 devices in a mesh: sweep: 4 (over y, core), layer: 8 (over z, x).
Axes of the slice: x: 2, y: 2, z: 4, core: 2. Of those that a mesh axis runs over, the one named last changes fastest.
Arguments:
- face_rhs: float32 [4, 16, 32, 384], P('sweep', None, 'layer'), may hold values from -6 to 6
- res_rows: float32 [16384, 384], P(('sweep', 'layer')), may hold values from -4 to 4
- row_owner: int32 [16384, 1], P(('sweep', 'layer')), may hold values from 0 to 7; in each aligned block of 512 rows (0 to 511, 512 to 1023, ...) at most 128 rows name the same one
- row_slot: int32 [16384], P(('sweep', 'layer')), may hold values from 0 to 63
- inv_blocks: bfloat16 [4, 32, 384, 384], P('sweep', 'layer'), may hold values from -0.3125 to 0.3125
- couple_in: bfloat16 [4, 1536, 12288], P('sweep', None, 'layer'), may hold values from -0.15625 to 0.15625
- couple_out: bfloat16 [4, 12288, 1536], P('sweep', 'layer'), may hold values from -0.0546875 to 0.0546875
Outputs:
- solved: float32 [4, 16, 32, 384], P('sweep', None, 'layer')
The draws below stay inside these ranges and needn't reach their ends.
Inputs may be any that keep to these rules, and one draw needn't show every extreme that they name: `row_owner`: among the 512 rows of one device no owner is named by more than 128 rows, a bound that some block reaches.
All inputs are finite; a program needn't handle non-finite values.
Results may differ from the reference program's by a relative error of at most 0.02.
Values may be sent and summed in bfloat16 or wider, within the bound.
A program may use at most 64 MiB of HBM per device.

```python
import math
import jax
import jax.numpy as jnp
import numpy as np

W = 384
P_SIZE = 1536
R = 16
FACE_DEV = 4
ROW_DEV = 512
LAYERS = 4
FACES = 32
CAP = 128
ROWS = 16384
N_LAYER = 8


def plant(entries, key, least, top_value):
    spot = [jax.random.randint(jax.random.fold_in(key, axis), (), 0, length) for axis, length in enumerate(entries.shape)]
    widest = entries.shape.index(max(entries.shape))
    next_to = spot[:widest] + [(spot[widest] + 1) % entries.shape[widest]] + spot[widest + 1:]
    return entries.at[tuple(spot)].set(least).at[tuple(next_to)].set(top_value)


def shard_levels(stream_key, extent, split, least, high):
    loudness, own = 1.0, jax.random.fold_in(stream_key, 6)
    for position, blocks in split:
        steps = jnp.exp(jax.random.uniform(jax.random.fold_in(own, position), (blocks,), jnp.float32, least / len(split), high / len(split)))
        loudness = loudness * jnp.repeat(steps, extent[position] // blocks).reshape([-1 if axis == position else 1 for axis in range(len(extent))])
    return loudness


def deal_out(stream_key, own, number, rows, amount, top, reach, slope):
    order = jax.random.permutation(stream_key, amount)
    packed, usual = portions_of(amount, rows * top, reach, slope, True), portions_of(amount, rows * top, reach, slope, False)
    places = jnp.arange(amount)

    def named(lengths, rotation):
        used = int((lengths > 0).sum())
        fixed = max(1, used // 4)
        moved = fixed + (places - fixed + rotation * (used - fixed)) % max(1, amount - fixed)
        return jnp.zeros((amount,), jnp.int32).at[order[jnp.where(places < fixed, places, moved)]].set(jnp.asarray(lengths, jnp.int32))

    lengths = jnp.where(number % 4 == 0, named(packed, number // 4), named(usual, number - number // 4 - 1))
    mixed = jax.random.permutation(jax.random.fold_in(own, 3), amount)
    source_of, taker = mixed[0:amount // 2 * 2:2], mixed[1:amount // 2 * 2:2]
    slack = jnp.minimum(lengths[source_of] - 1, reach - lengths[taker]) // 2
    slack = jnp.where((source_of == order[0]) | (taker == order[0]) | (lengths[taker] == 0), 0, jnp.maximum(slack, 0))
    moved = jax.random.randint(jax.random.fold_in(own, 4), (amount // 2,), 0, 1 << 20) % (slack + 1)
    lengths = lengths.at[source_of].add(-moved).at[taker].add(moved)
    labels = jnp.searchsorted(jnp.cumsum(lengths), jnp.arange(rows * top), side="right").astype(jnp.int32)
    table = labels.reshape(top, rows).T
    table = table[jax.random.permutation(jax.random.fold_in(own, 1), rows)]
    rotation = jax.random.randint(jax.random.fold_in(own, 2), (rows, 1), 0, top)
    return jnp.take_along_axis(table, (jnp.arange(top)[None, :] + rotation) % top, axis=1)


def portions_of(number_of, total, bound, skew, full):
    loads = [(1 << 20) // math.isqrt(rank ** skew) + 1 for rank in range(1, number_of + 1)]
    largest = bound if full else min(bound, max(-(-total // number_of), total * loads[0] // sum(loads)))
    least = 1 if total - largest >= number_of - 1 else 0
    holding, surplus = [largest] + [least] * (number_of - 1), total - largest - least * (number_of - 1)
    while surplus > 0:
        candidates = [i for i in range(1, number_of) if holding[i] < largest] or [i for i in range(1, number_of) if holding[i] < bound]
        pool, budget = sum([loads[i] for i in candidates]), surplus
        for i in candidates:
            extra = min(bound - holding[i], max(1, budget * loads[i] // pool), surplus)
            holding[i] = holding[i] + extra
            surplus = surplus - extra
    return np.array(holding)


def scatter_about(rng, dims, width, most, shards=(), kind=jnp.bfloat16):
    array = jax.random.normal(rng, dims, jnp.float32) * width
    if len(shards) > 0:
        array = shard_levels(rng, dims, shards, -0.22, 0.18) * array
    return jnp.clip(array, min=-most, max=most).astype(kind)


def setup_inputs(seed: int = 0) -> dict:
    splits = jax.random.split(jax.random.key(seed), 8)
    face_rhs = scatter_about(splits[0], (LAYERS, R, FACES, W), 1.0, 6.0, ((0, 4), (2, 8)), jnp.float32)
    res_rows = scatter_about(splits[1], (ROWS, W), 0.5, 4.0, ((0, 32),), jnp.float32)
    row_owner_keys = jax.random.split(jax.random.fold_in(splits[2], 1), ROWS // ROW_DEV)
    row_owner_turns = jax.random.permutation(jax.random.fold_in(splits[2], 3), ROWS // ROW_DEV)
    row_owner = jax.vmap(lambda own, number: deal_out(jax.random.fold_in(splits[2], 2), own, number, ROW_DEV, N_LAYER, 1, CAP, 2))(row_owner_keys, row_owner_turns).reshape((ROWS, 1))
    row_slot = plant(jax.random.randint(splits[3], (ROWS,), 0, FACE_DEV * R), jax.random.fold_in(splits[3], 1), 0, (FACE_DEV * R) - 1).astype(jnp.int32)
    inv_blocks = scatter_about(splits[4], (LAYERS, FACES, W, W), W ** -0.5, 0.3125, ((0, 4), (1, 8)))
    couple_in = scatter_about(splits[5], (LAYERS, P_SIZE, FACES * W), P_SIZE ** -0.5, 0.15625, ((0, 4), (2, 8)))
    couple_out = scatter_about(splits[6], (LAYERS, FACES * W, P_SIZE), (FACES * W) ** -0.5, 0.0546875, ((0, 4), (1, 8)))
    return dict(face_rhs=face_rhs, res_rows=res_rows, row_owner=row_owner, row_slot=row_slot, inv_blocks=inv_blocks, couple_in=couple_in, couple_out=couple_out)


def reference(face_rhs, res_rows, row_owner, row_slot, inv_blocks, couple_in, couple_out):
    row_index = jnp.arange(ROWS, dtype=jnp.int32)
    layer_of_row = row_index // (ROW_DEV * N_LAYER)
    rhs_of_row = row_slot // FACE_DEV
    face_of_row = row_owner[:, 0] * FACE_DEV + row_slot % FACE_DEV
    target = ((layer_of_row * R + rhs_of_row) * FACES + face_of_row).astype(jnp.int32)
    added_rows = jax.ops.segment_sum(res_rows, target, num_segments=LAYERS * R * FACES)
    assembled = face_rhs + added_rows.reshape(LAYERS, R, FACES, W)
    panel_in = jnp.zeros((R, P_SIZE), jnp.float32)
    results = []
    for layer_step in range(LAYERS):
        coupled = jnp.dot(panel_in.astype(jnp.bfloat16), couple_in[layer_step], preferred_element_type=jnp.float32)
        local_part = (assembled[layer_step] - coupled.reshape(R, FACES, W)).astype(jnp.bfloat16)
        solved = jnp.einsum("rfw,fwv->rfv", local_part.astype(jnp.float32), inv_blocks[layer_step].astype(jnp.float32))
        results.append(solved)
        flattened = solved.astype(jnp.bfloat16).reshape(R, FACES * W)
        panel_in = jnp.dot(flattened, couple_out[layer_step], preferred_element_type=jnp.float32)
    return jnp.stack(results)
```

```python
import functools

import jax
import jax.numpy as jnp
from jax import lax
from jax.experimental import pallas as pl
from jax.experimental.pallas import tpu as pltpu
from jax.sharding import PartitionSpec as P

MESH = pl.DeviceIdType.MESH
F32 = jnp.float32
BF16 = jnp.bfloat16
SLICE = 256


def dot(a, b):
    return jnp.dot(a, b, preferred_element_type=F32)


def kernel(
    n, layers, deep_from,
    owner_ref, slot_ref, rows_ref, face_ref, inv_ref, cin_ref, cout_ref,
    out_ref,
    owner_v, slot_v, rows_v, face_v, inv_v, cin_v, cout_v, wide_v, deep_v,
    send_v, recv_v, part_sum_v, base_v, acc_v, pan_v, part_v, prec_v,
    load_sem, a_send, a_recv, r_send, r_recv, g_send, g_recv,
):
    s = lax.axis_index("sweep")
    i = lax.axis_index("layer")
    rhs, faces, w = face_v.shape
    slots = rhs * faces
    panel = cin_v.shape[0]
    own_w = faces * w
    pieces = panel // SLICE
    low = (n - pieces) // 2
    half = faces // 2
    half_rows = half * rhs
    half_w = half * w
    mine = i - low
    sums = (mine >= 0) & (mine < pieces)
    first, last = s == 0, s == layers - 1
    deep = (s >= deep_from) & (s < layers - 1)

    barrier = pltpu.get_barrier_semaphore()
    for k in range(1, n):
        pl.semaphore_signal(
            barrier, inc=1, device_id=(s, lax.rem(i + k, n)), device_id_type=MESH
        )

    @pl.when((s > 0) & sums)
    def _():
        for k in range(n):
            pl.semaphore_signal(
                barrier, inc=1, device_id=(s - 1, lax.rem(i + k, n)), device_id_type=MESH
            )

    def load(src, dst, index):
        return pltpu.make_async_copy(src, dst, load_sem.at[index])

    third = panel // 3
    load_owner = load(owner_ref, owner_v, 0)
    load_slot = load(slot_ref, slot_v, 1)
    load_rows = load(rows_ref, rows_v, 2)
    load_face = load(face_ref.at[0], face_v, 3)
    load_inv = load(inv_ref.at[0], inv_v, 4)
    load_out = load(cout_ref.at[0], cout_v, 5)
    load_in = [
        load(cin_ref.at[0, pl.ds(b * third, third)], cin_v.at[pl.ds(b * third, third)], 6 + b)
        for b in range(3)
    ]
    for copy in (load_owner, load_slot, load_rows, load_inv, load_face):
        copy.start()

    @pl.when(jnp.logical_not(first))
    def _():
        for copy in load_in:
            copy.start()

    load_out.start()

    load_owner.wait()
    load_slot.wait()
    slot = slot_v[...]
    target = owner_v[...] * slots + (slot % faces) * rhs + slot // faces
    load_rows.wait()
    rows = rows_v[...].astype(BF16)
    group = 4
    for g in range(0, n, group):
        place = lax.broadcasted_iota(jnp.int32, (group * slots, rows.shape[0]), 0) + g * slots
        hot = jnp.where(place == target, 1.0, 0.0).astype(BF16)
        summed = dot(hot, rows).astype(BF16)
        for j in range(group):
            send_v[g + j] = summed[j * slots : (j + 1) * slots]

    heard = (n - 1) + jnp.where(last, 0, pieces)
    pl.semaphore_wait(barrier, heard)

    def row_copy(k, q):
        to = lax.rem(i + k, n)
        part = pl.ds(q * half_rows, half_rows)
        return pltpu.make_async_remote_copy(
            src_ref=send_v.at[to, part],
            dst_ref=recv_v.at[i, part],
            send_sem=a_send.at[k, q],
            recv_sem=a_recv.at[i, q],
            device_id=(s, to),
            device_id_type=MESH,
        )

    def row_arrival(source, q):
        part = pl.ds(q * half_rows, half_rows)
        return pltpu.make_async_remote_copy(
            src_ref=send_v.at[source, part],
            dst_ref=recv_v.at[source, part],
            send_sem=a_send.at[0, q],
            recv_sem=a_recv.at[source, q],
            device_id=(s, source),
            device_id_type=MESH,
        )

    def send_rows():
        for q in range(2):
            for k in range(1, n):
                row_copy(k, q).start()

    def panel_copy(c):
        return pltpu.make_async_remote_copy(
            src_ref=part_v.at[c],
            dst_ref=prec_v.at[i],
            send_sem=r_send.at[c],
            recv_sem=r_recv.at[i],
            device_id=(s + 1, low + c),
            device_id_type=MESH,
        )

    def send_panel(c, value):
        part_v[c] = value.astype(BF16)
        panel_copy(c).start()

    def columns(c):
        return slice(c * SLICE, (c + 1) * SLICE)

    def assemble(q):
        for k in range(1, n):
            row_arrival(lax.rem(i + k, n), q).wait_recv()
        for f in range(q * half, (q + 1) * half):
            part = slice(f * rhs, (f + 1) * rhs)
            total = face_v[:, f, :] + send_v[i, part, :].astype(F32)
            for k in range(1, n):
                total = total + recv_v[lax.rem(i + k, n), part, :].astype(F32)
            local = total.astype(BF16)
            cols = slice(f * w, (f + 1) * w)
            acc_v[:, cols] = total
            base_v[:, cols] = dot(local, inv_v[f])

    @pl.when(jnp.logical_not(s == 1))
    def _():
        send_rows()

    load_inv.wait()
    load_face.wait()

    @pl.when(first)
    def _():
        load_out.wait()
        assemble(0)
        head = base_v[:, :half_w].astype(BF16)
        for c in range(pieces):
            part_sum_v[:, columns(c)] = dot(head, cout_v[:half_w, columns(c)])
        assemble(1)
        tail = base_v[:, half_w:].astype(BF16)
        for c in range(pieces):
            send_panel(c, part_sum_v[:, columns(c)] + dot(tail, cout_v[half_w:, columns(c)]))
        out_ref[...] = base_v[...]

    def wait_in():
        for copy in load_in:
            copy.wait()

    def arrive(c):
        @pl.when(mine != c)
        def _():
            pltpu.make_async_remote_copy(
                src_ref=pan_v.at[c],
                dst_ref=pan_v.at[c],
                send_sem=g_send.at[0],
                recv_sem=g_recv.at[c],
                device_id=(s, low + c),
                device_id_type=MESH,
            ).wait_recv()

    def spread_copy(k):
        return pltpu.make_async_remote_copy(
            src_ref=pan_v.at[mine],
            dst_ref=pan_v.at[mine],
            send_sem=g_send.at[k],
            recv_sem=g_recv.at[mine],
            device_id=(s, lax.rem(i + k, n)),
            device_id_type=MESH,
        )

    def sum_panel():
        @pl.when(sums)
        def _():
            total = None
            for j in range(n):
                pltpu.make_async_remote_copy(
                    src_ref=part_v.at[0],
                    dst_ref=prec_v.at[j],
                    send_sem=r_send.at[0],
                    recv_sem=r_recv.at[j],
                    device_id=(s, j),
                    device_id_type=MESH,
                ).wait_recv()
                value = prec_v[j].astype(F32)
                total = value if total is None else total + value
            pan_v[mine] = total.astype(BF16)
            for k in range(1, n):
                spread_copy(k).start()

    @pl.when(jnp.logical_not(first) & jnp.logical_not(deep))
    def _():
        for b in range(3):
            load_in[b].wait()
            part = slice(b * third, (b + 1) * third)
            for f in range(faces):
                cols = slice(f * w, (f + 1) * w)
                wide_v[part, cols] = dot(cin_v[part, cols], inv_v[f]).astype(BF16)

        @pl.when(s == 1)
        def _():
            send_rows()

        load_out.wait()
        assemble(0)
        assemble(1)
        sum_panel()
        for c in range(pieces):
            arrive(c)
            product = dot(pan_v[c], wide_v[columns(c), :])
            if c == 0:
                acc_v[...] = base_v[...] - product
            else:
                acc_v[...] = acc_v[...] - product
        solved = acc_v[...]
        out_ref[...] = solved

        @pl.when(jnp.logical_not(last))
        def _():
            flat = acc_v[...].astype(BF16)
            for c in range(pieces):
                send_panel(c, dot(flat, cout_v[:, columns(c)]))

    @pl.when(deep)
    def _():
        load_out.wait()

        @pl.loop(0, own_w // 512)
        def _(b):
            cols = pl.ds(pl.multiple_of(b * 512, 512), 512)
            for f in range(faces):
                part = slice(f * w, (f + 1) * w)
                wide_v[part, cols] = dot(inv_v[f], cout_v[part, cols]).astype(BF16)

        wait_in()

        @pl.loop(0, panel // SLICE)
        def _(b):
            cols = pl.ds(pl.multiple_of(b * SLICE, SLICE), SLICE)
            deep_v[:, cols] = dot(cin_v[...], wide_v[:, cols]).astype(BF16)

        assemble(0)
        assemble(1)
        kept = acc_v[...]
        out_ref[...] = kept
        flat = base_v[...].astype(BF16)
        for c in range(pieces):
            acc_v[:, columns(c)] = dot(flat, cout_v[:, columns(c)])
        sum_panel()
        for c in range(pieces - 1):
            arrive(c)
            acc_v[...] = acc_v[...] - dot(pan_v[c], deep_v[columns(c), :])
        arrive(pieces - 1)
        tail = pan_v[pieces - 1]
        for c in range(pieces):
            send_panel(c, acc_v[:, columns(c)] - dot(tail, deep_v[columns(pieces - 1), columns(c)]))
        for c in range(pieces):
            out_ref[...] = out_ref[...] - dot(pan_v[c], cin_v[columns(c), :])
        for f in range(faces):
            cols = slice(f * w, (f + 1) * w)
            out_ref[:, cols] = dot(out_ref[:, cols].astype(BF16), inv_v[f])

    for q in range(2):
        for k in range(1, n):
            row_copy(k, q).wait_send()

    @pl.when(jnp.logical_not(last))
    def _():
        for c in range(pieces):
            panel_copy(c).wait_send()

    @pl.when(jnp.logical_not(first) & sums)
    def _():
        for k in range(1, n):
            spread_copy(k).wait_send()


def on_device(
    n, layers, face_rhs, res_rows, row_owner, row_slot, inv_blocks, couple_in, couple_out
):
    _, rhs, faces, w = face_rhs.shape
    count = res_rows.shape[0]
    panel, own_w = couple_in.shape[1:]
    pieces = panel // SLICE
    any_ref = pl.BlockSpec(memory_space=pl.ANY)
    solved = pl.pallas_call(
        functools.partial(kernel, n, layers, 2),
        out_shape=jax.ShapeDtypeStruct((rhs, own_w), F32),
        in_specs=[any_ref] * 7,
        out_specs=pl.BlockSpec(memory_space=pltpu.VMEM),
        scratch_shapes=[
            pltpu.VMEM((1, count), jnp.int32),
            pltpu.VMEM((1, count), jnp.int32),
            pltpu.VMEM((count, w), F32),
            pltpu.VMEM((rhs, faces, w), F32),
            pltpu.VMEM((faces, w, w), BF16),
            pltpu.VMEM((panel, own_w), BF16),
            pltpu.VMEM((own_w, panel), BF16),
            pltpu.VMEM((panel, own_w), BF16),
            pltpu.VMEM((panel, panel), BF16),
            pltpu.VMEM((n, rhs * faces, w), BF16),
            pltpu.VMEM((n, rhs * faces, w), BF16),
            pltpu.VMEM((rhs, panel), F32),
            pltpu.VMEM((rhs, own_w), F32),
            pltpu.VMEM((rhs, panel), F32),
            pltpu.VMEM((pieces, rhs, SLICE), BF16),
            pltpu.VMEM((pieces, rhs, SLICE), BF16),
            pltpu.VMEM((n, rhs, SLICE), BF16),
            pltpu.SemaphoreType.DMA((9,)),
            pltpu.SemaphoreType.DMA((n, 2)),
            pltpu.SemaphoreType.DMA((n, 2)),
            pltpu.SemaphoreType.DMA((pieces,)),
            pltpu.SemaphoreType.DMA((n,)),
            pltpu.SemaphoreType.DMA((n,)),
            pltpu.SemaphoreType.DMA((pieces,)),
        ],
        compiler_params=pltpu.CompilerParams(
            collective_id=0, has_side_effects=True, vmem_limit_bytes=50 * 1024 * 1024
        ),
    )(
        row_owner.reshape(1, count),
        row_slot.reshape(1, count),
        res_rows,
        face_rhs,
        inv_blocks,
        couple_in,
        couple_out,
    )
    return solved.reshape(1, rhs, faces, w)


def solution(mesh):
    return jax.shard_map(
        functools.partial(on_device, mesh.shape["layer"], mesh.shape["sweep"]),
        mesh=mesh,
        in_specs=(
            P("sweep", None, "layer", None),
            P(("sweep", "layer"), None),
            P(("sweep", "layer"), None),
            P(("sweep", "layer")),
            P("sweep", "layer", None, None),
            P("sweep", None, "layer"),
            P("sweep", "layer", None),
        ),
        out_specs=P("sweep", None, "layer", None),
        check_vma=False,
    )
```

```python
import functools

import jax
import jax.numpy as jnp
from jax import lax
from jax.experimental import pallas as pl
from jax.experimental.pallas import tpu as pltpu
from jax.sharding import PartitionSpec as P

MESH = pl.DeviceIdType.MESH
F32 = jnp.float32
BF16 = jnp.bfloat16
OWNERS = 4


def dot(a, b):
    return jnp.dot(a, b, preferred_element_type=F32)


def kernel(
    n, layers, deep_from,
    owner_ref, slot_ref, rows_ref, face_ref, inv_ref, cin_ref, cout_ref,
    out_ref,
    owner_v, slot_v, rows_v, face_v, inv_v, cin_v, cout_v, wide_v, deep_v,
    send_v, recv_v, part_sum_v, base_v, acc_v, pan_v, part_v, prec_v,
    load_sem, a_send, a_recv, r_send, r_recv, g_send, g_recv,
):
    s = lax.axis_index("sweep")
    i = lax.axis_index("layer")
    rhs, faces, w = face_v.shape
    slots = rhs * faces
    panel = cin_v.shape[0]
    own_w = faces * w
    pieces = OWNERS
    width = panel // pieces
    pair = 2 * width
    low = (n - pieces) // 2
    near = jnp.where(i < n // 2, 0, 1)
    half = faces // 2
    half_rows = half * rhs
    half_w = half * w
    mine = i - low
    sums = (mine >= 0) & (mine < pieces)
    first, last = s == 0, s == layers - 1
    deep = (s >= deep_from) & (s < layers - 1)

    def load(src, dst, index):
        return pltpu.make_async_copy(src, dst, load_sem.at[index])

    third = panel // 3
    load_owner = load(owner_ref, owner_v, 0)
    load_slot = load(slot_ref, slot_v, 1)
    load_rows = load(rows_ref, rows_v, 2)
    load_face = load(face_ref.at[0], face_v, 3)
    load_inv = load(inv_ref.at[0], inv_v, 4)
    load_out = load(cout_ref.at[0], cout_v, 5)
    load_in = [
        load(cin_ref.at[0, pl.ds(b * third, third)], cin_v.at[pl.ds(b * third, third)], 6 + b)
        for b in range(3)
    ]
    for copy in (load_owner, load_slot, load_rows, load_inv, load_face):
        copy.start()

    @pl.when(jnp.logical_not(first))
    def _():
        for copy in load_in:
            copy.start()

    load_out.start()

    barrier = pltpu.get_barrier_semaphore()
    for k in range(1, n):
        pl.semaphore_signal(
            barrier, inc=1, device_id=(s, lax.rem(i + k, n)), device_id_type=MESH
        )

    @pl.when((s > 0) & sums)
    def _():
        for k in range(n):
            pl.semaphore_signal(
                barrier, inc=1, device_id=(s - 1, lax.rem(i + k, n)), device_id_type=MESH
            )

    load_owner.wait()
    load_slot.wait()
    slot = slot_v[...]
    target = owner_v[...] * slots + (slot % faces) * rhs + slot // faces
    load_rows.wait()
    rows = rows_v[...].astype(BF16)
    group = 4
    for g in range(0, n, group):
        place = lax.broadcasted_iota(jnp.int32, (group * slots, rows.shape[0]), 0) + g * slots
        hot = jnp.where(place == target, 1.0, 0.0).astype(BF16)
        summed = dot(hot, rows).astype(BF16)
        for j in range(group):
            send_v[g + j] = summed[j * slots : (j + 1) * slots]

    heard = (n - 1) + jnp.where(last, 0, pieces)
    pl.semaphore_wait(barrier, heard)

    def row_copy(k, q):
        to = lax.rem(i + k, n)
        part = pl.ds(q * half_rows, half_rows)
        return pltpu.make_async_remote_copy(
            src_ref=send_v.at[to, part],
            dst_ref=recv_v.at[i, part],
            send_sem=a_send.at[k, q],
            recv_sem=a_recv.at[i, q],
            device_id=(s, to),
            device_id_type=MESH,
        )

    def row_arrival(source, q):
        part = pl.ds(q * half_rows, half_rows)
        return pltpu.make_async_remote_copy(
            src_ref=send_v.at[source, part],
            dst_ref=recv_v.at[source, part],
            send_sem=a_send.at[0, q],
            recv_sem=a_recv.at[source, q],
            device_id=(s, source),
            device_id_type=MESH,
        )

    def send_rows():
        for q in range(2):
            for k in range(1, n):
                row_copy(k, q).start()

    def panel_copy(c):
        return pltpu.make_async_remote_copy(
            src_ref=part_v.at[c],
            dst_ref=prec_v.at[i],
            send_sem=r_send.at[c],
            recv_sem=r_recv.at[i],
            device_id=(s + 1, low + c),
            device_id_type=MESH,
        )

    def send_panel(c, value):
        part_v[c] = value.astype(BF16)
        panel_copy(c).start()

    def columns(h):
        return slice(h * pair, (h + 1) * pair)

    def send_pair(h, value):
        for a in range(2):
            send_panel(2 * h + a, value[:, a * width : (a + 1) * width])

    def assemble(q):
        for k in range(1, n):
            row_arrival(lax.rem(i + k, n), q).wait_recv()
        for f in range(q * half, (q + 1) * half):
            part = slice(f * rhs, (f + 1) * rhs)
            total = face_v[:, f, :] + send_v[i, part, :].astype(F32)
            for k in range(1, n):
                total = total + recv_v[lax.rem(i + k, n), part, :].astype(F32)
            local = total.astype(BF16)
            cols = slice(f * w, (f + 1) * w)
            acc_v[:, cols] = total
            base_v[:, cols] = dot(local, inv_v[f])

    @pl.when(jnp.logical_not(s == 1))
    def _():
        send_rows()

    load_inv.wait()
    load_face.wait()

    @pl.when(first)
    def _():
        load_out.wait()
        assemble(0)
        head = base_v[:, :half_w].astype(BF16)
        part_sum_v[...] = dot(head, cout_v[:half_w, :])
        assemble(1)
        tail = base_v[:, half_w:].astype(BF16)
        for h in range(2):
            send_pair(h, part_sum_v[:, columns(h)] + dot(tail, cout_v[half_w:, columns(h)]))
        out_ref[...] = base_v[...]

    def wait_in():
        for copy in load_in:
            copy.wait()

    def arrive(c):
        @pl.when(mine != c)
        def _():
            pltpu.make_async_remote_copy(
                src_ref=pan_v.at[c],
                dst_ref=pan_v.at[c],
                send_sem=g_send.at[0],
                recv_sem=g_recv.at[c],
                device_id=(s, low + c),
                device_id_type=MESH,
            ).wait_recv()

    def arrived_pair(h):
        for a in range(2):
            arrive(2 * h + a)
        return jnp.concatenate([pan_v[2 * h], pan_v[2 * h + 1]], axis=1)

    def pair_rows(h):
        return pl.ds(pl.multiple_of(h * pair, pair), pair)

    def spread_copy(k):
        return pltpu.make_async_remote_copy(
            src_ref=pan_v.at[mine],
            dst_ref=pan_v.at[mine],
            send_sem=g_send.at[k],
            recv_sem=g_recv.at[mine],
            device_id=(s, lax.rem(i + k, n)),
            device_id_type=MESH,
        )

    def sum_panel():
        @pl.when(sums)
        def _():
            total = None
            for j in range(n):
                pltpu.make_async_remote_copy(
                    src_ref=part_v.at[0],
                    dst_ref=prec_v.at[j],
                    send_sem=r_send.at[0],
                    recv_sem=r_recv.at[j],
                    device_id=(s, j),
                    device_id_type=MESH,
                ).wait_recv()
                value = prec_v[j].astype(F32)
                total = value if total is None else total + value
            pan_v[mine] = total.astype(BF16)
            for k in range(1, n):
                spread_copy(k).start()

    @pl.when(jnp.logical_not(first) & jnp.logical_not(deep))
    def _():
        for b in range(3):
            load_in[b].wait()
            part = slice(b * third, (b + 1) * third)
            for f in range(faces):
                cols = slice(f * w, (f + 1) * w)
                wide_v[part, cols] = dot(cin_v[part, cols], inv_v[f]).astype(BF16)

        load_out.wait()
        assemble(0)
        assemble(1)
        sum_panel()
        acc_v[...] = base_v[...] - dot(arrived_pair(near), wide_v[pair_rows(near), :])
        far = 1 - near
        solved = acc_v[...] - dot(arrived_pair(far), wide_v[pair_rows(far), :])
        out_ref[...] = solved

        @pl.when(jnp.logical_not(last))
        def _():
            flat = out_ref[...].astype(BF16)
            for h in range(2):
                send_pair(h, dot(flat, cout_v[:, columns(h)]))

    @pl.when(deep)
    def _():
        load_out.wait()

        @pl.loop(0, own_w // 512)
        def _(b):
            cols = pl.ds(pl.multiple_of(b * 512, 512), 512)
            for f in range(faces):
                part = slice(f * w, (f + 1) * w)
                wide_v[part, cols] = dot(inv_v[f], cout_v[part, cols]).astype(BF16)

        @pl.when(s == 1)
        def _():
            send_rows()

        wait_in()

        @pl.loop(0, panel // 256)
        def _(b):
            cols = pl.ds(pl.multiple_of(b * 256, 256), 256)
            deep_v[:, cols] = dot(cin_v[...], wide_v[:, cols]).astype(BF16)

        assemble(0)
        assemble(1)
        kept = acc_v[...]
        out_ref[...] = kept
        flat = base_v[...].astype(BF16)
        acc_v[...] = dot(flat, cout_v[...])
        sum_panel()
        acc_v[...] = acc_v[...] - dot(arrived_pair(near), deep_v[pair_rows(near), :])
        far = 1 - near
        rest = arrived_pair(far)
        for h in range(2):
            send_pair(h, acc_v[:, columns(h)] - dot(rest, deep_v[pair_rows(far), columns(h)]))
        whole = jnp.concatenate([pan_v[c] for c in range(pieces)], axis=1)
        out_ref[...] = out_ref[...] - dot(whole, cin_v[...])
        for f in range(faces):
            cols = slice(f * w, (f + 1) * w)
            out_ref[:, cols] = dot(out_ref[:, cols].astype(BF16), inv_v[f])

    for q in range(2):
        for k in range(1, n):
            row_copy(k, q).wait_send()

    @pl.when(jnp.logical_not(last))
    def _():
        for c in range(pieces):
            panel_copy(c).wait_send()

    @pl.when(jnp.logical_not(first) & sums)
    def _():
        for k in range(1, n):
            spread_copy(k).wait_send()


def on_device(
    n, layers, face_rhs, res_rows, row_owner, row_slot, inv_blocks, couple_in, couple_out
):
    _, rhs, faces, w = face_rhs.shape
    count = res_rows.shape[0]
    panel, own_w = couple_in.shape[1:]
    pieces, width = OWNERS, panel // OWNERS
    any_ref = pl.BlockSpec(memory_space=pltpu.HBM)
    solved = pl.pallas_call(
        functools.partial(kernel, n, layers, 1),
        out_shape=jax.ShapeDtypeStruct((rhs, own_w), F32),
        in_specs=[any_ref] * 7,
        out_specs=pl.BlockSpec(memory_space=pltpu.VMEM),
        scratch_shapes=[
            pltpu.VMEM((1, count), jnp.int32),
            pltpu.VMEM((1, count), jnp.int32),
            pltpu.VMEM((count, w), F32),
            pltpu.VMEM((rhs, faces, w), F32),
            pltpu.VMEM((faces, w, w), BF16),
            pltpu.VMEM((panel, own_w), BF16),
            pltpu.VMEM((own_w, panel), BF16),
            pltpu.VMEM((panel, own_w), BF16),
            pltpu.VMEM((panel, panel), BF16),
            pltpu.VMEM((n, rhs * faces, w), BF16),
            pltpu.VMEM((n, rhs * faces, w), BF16),
            pltpu.VMEM((rhs, panel), F32),
            pltpu.VMEM((rhs, own_w), F32),
            pltpu.VMEM((rhs, panel), F32),
            pltpu.VMEM((pieces, rhs, width), BF16),
            pltpu.VMEM((pieces, rhs, width), BF16),
            pltpu.VMEM((n, rhs, width), BF16),
            pltpu.SemaphoreType.DMA((9,)),
            pltpu.SemaphoreType.DMA((n, 2)),
            pltpu.SemaphoreType.DMA((n, 2)),
            pltpu.SemaphoreType.DMA((pieces,)),
            pltpu.SemaphoreType.DMA((n,)),
            pltpu.SemaphoreType.DMA((n,)),
            pltpu.SemaphoreType.DMA((pieces,)),
        ],
        compiler_params=pltpu.CompilerParams(
            collective_id=0, has_side_effects=True, vmem_limit_bytes=63 * 1024 * 1024
        ),
    )(
        row_owner.reshape(1, count),
        row_slot.reshape(1, count),
        res_rows,
        face_rhs,
        inv_blocks,
        couple_in,
        couple_out,
    )
    return solved.reshape(1, rhs, faces, w)


def solution(mesh):
    return jax.shard_map(
        functools.partial(on_device, mesh.shape["layer"], mesh.shape["sweep"]),
        mesh=mesh,
        in_specs=(
            P("sweep", None, "layer", None),
            P(("sweep", "layer"), None),
            P(("sweep", "layer"), None),
            P(("sweep", "layer")),
            P("sweep", "layer", None, None),
            P("sweep", None, "layer"),
            P("sweep", "layer", None),
        ),
        out_specs=P("sweep", None, "layer", None),
        check_vma=False,
    )
```

```python
import functools

import jax
import jax.numpy as jnp
from jax import lax
from jax.experimental import pallas as pl
from jax.experimental.pallas import tpu as pltpu
from jax.sharding import PartitionSpec as P

MESH = pl.DeviceIdType.MESH
F32 = jnp.float32
BF16 = jnp.bfloat16
OWNERS = 4


def dot(a, b):
    return jnp.dot(a, b, preferred_element_type=F32)


def kernel(
    n, layers,
    owner_ref, slot_ref, rows_ref, face_ref, inv_ref, cin_ref, cout_ref,
    out_ref,
    owner_v, slot_v, rows_v, face_v, inv_v, cin_v, cout_v, wide_v, deep_v,
    send_v, recv_v, full_v, local_v, acc_v, out_v, pan_v, part_v, prec_v,
    load_sem, a_send, a_recv, r_send, r_recv, g_send, g_recv,
):
    s = lax.axis_index("sweep")
    i = lax.axis_index("layer")
    rhs, faces, w = face_v.shape
    slots = rhs * faces
    panel = cin_v.shape[0]
    own_w = faces * w
    pieces = OWNERS
    width = panel // pieces
    pair = 2 * width
    low = (n - pieces) // 2
    half = faces // 2
    half_rows = half * rhs
    half_w = half * w
    mine = i - low
    sums = (mine >= 0) & (mine < pieces)
    first, last = s == 0, s == layers - 1

    def load(src, dst, index):
        return pltpu.make_async_copy(src, dst, load_sem.at[index])

    third = panel // 3
    load_owner = load(owner_ref, owner_v, 0)
    load_slot = load(slot_ref, slot_v, 1)
    load_rows = load(rows_ref, rows_v, 2)
    load_face = load(face_ref.at[0], face_v, 3)
    load_inv = load(inv_ref.at[0], inv_v, 4)
    load_out = load(cout_ref.at[0], cout_v, 5)
    load_in = [
        load(cin_ref.at[0, pl.ds(b * third, third)], cin_v.at[pl.ds(b * third, third)], 6 + b)
        for b in range(3)
    ]
    for copy in (load_owner, load_slot, load_rows):
        copy.start()

    barrier = pltpu.get_barrier_semaphore()
    for k in range(1, n):
        pl.semaphore_signal(
            barrier, inc=1, device_id=(s, lax.rem(i + k, n)), device_id_type=MESH
        )

    @pl.when((s > 0) & sums)
    def _():
        for k in range(n):
            pl.semaphore_signal(
                barrier, inc=1, device_id=(s - 1, lax.rem(i + k, n)), device_id_type=MESH
            )

    load_owner.wait()
    load_slot.wait()
    slot = slot_v[...]
    target = owner_v[...] * slots + (slot % faces) * rhs + slot // faces
    load_rows.wait()
    load_inv.start()

    @pl.when(last)
    def _():
        for copy in load_in:
            copy.start()

    @pl.when(jnp.logical_not(last))
    def _():
        load_out.start()

    load_face.start()

    @pl.when(jnp.logical_not(first | last))
    def _():
        for copy in load_in:
            copy.start()

    rows = rows_v[...].astype(BF16)
    group = 4
    for g in range(0, n, group):
        place = lax.broadcasted_iota(jnp.int32, (group * slots, rows.shape[0]), 0) + g * slots
        hot = jnp.where(place == target, 1.0, 0.0).astype(BF16)
        summed = dot(hot, rows).astype(BF16)
        for j in range(group):
            send_v[g + j] = summed[j * slots : (j + 1) * slots]

    heard = (n - 1) + jnp.where(last, 0, pieces)
    pl.semaphore_wait(barrier, heard)

    def row_copy(k, q):
        to = lax.rem(i + k, n)
        part = pl.ds(q * half_rows, half_rows)
        return pltpu.make_async_remote_copy(
            src_ref=send_v.at[to, part],
            dst_ref=recv_v.at[i, part],
            send_sem=a_send.at[k, q],
            recv_sem=a_recv.at[i, q],
            device_id=(s, to),
            device_id_type=MESH,
        )

    def row_arrival(source, q):
        part = pl.ds(q * half_rows, half_rows)
        return pltpu.make_async_remote_copy(
            src_ref=send_v.at[source, part],
            dst_ref=recv_v.at[source, part],
            send_sem=a_send.at[0, q],
            recv_sem=a_recv.at[source, q],
            device_id=(s, source),
            device_id_type=MESH,
        )

    def send_rows():
        for q in range(2):
            for k in range(1, n):
                row_copy(k, q).start()

    def panel_copy(c):
        return pltpu.make_async_remote_copy(
            src_ref=part_v.at[c],
            dst_ref=prec_v.at[i],
            send_sem=r_send.at[c],
            recv_sem=r_recv.at[i],
            device_id=(s + 1, low + c),
            device_id_type=MESH,
        )

    def send_panel(c, value):
        part_v[c] = value.astype(BF16)
        panel_copy(c).start()

    def columns(h):
        return slice(h * pair, (h + 1) * pair)

    def send_pair(h, value):
        for a in range(2):
            send_panel(2 * h + a, value[:, a * width : (a + 1) * width])

    def assemble(q):
        for k in range(1, n):
            row_arrival(lax.rem(i + k, n), q).wait_recv()
        for f in range(q * half, (q + 1) * half):
            part = slice(f * rhs, (f + 1) * rhs)
            total = face_v[:, f, :] + send_v[i, part, :].astype(F32)
            for k in range(1, n):
                total = total + recv_v[lax.rem(i + k, n), part, :].astype(F32)
            local = total.astype(BF16)
            cols = slice(f * w, (f + 1) * w)
            full_v[:, cols] = total
            local_v[:, cols] = local

    @pl.when(jnp.logical_not(s == 1))
    def _():
        send_rows()

    load_inv.wait()
    load_face.wait()

    def wait_in():
        for copy in load_in:
            copy.wait()

    def arrive(c):
        @pl.when(mine != c)
        def _():
            pltpu.make_async_remote_copy(
                src_ref=pan_v.at[c],
                dst_ref=pan_v.at[c],
                send_sem=g_send.at[0],
                recv_sem=g_recv.at[c],
                device_id=(s, low + c),
                device_id_type=MESH,
            ).wait_recv()

    def arrived_pair(h):
        for a in range(2):
            arrive(2 * h + a)
        return jnp.concatenate([pan_v[2 * h], pan_v[2 * h + 1]], axis=1)

    def spread_copy(k):
        return pltpu.make_async_remote_copy(
            src_ref=pan_v.at[mine],
            dst_ref=pan_v.at[mine],
            send_sem=g_send.at[k],
            recv_sem=g_recv.at[mine],
            device_id=(s, lax.rem(i + k, n)),
            device_id_type=MESH,
        )

    def sum_panel():
        @pl.when(sums)
        def _():
            total = None
            for j in range(n):
                pltpu.make_async_remote_copy(
                    src_ref=part_v.at[0],
                    dst_ref=prec_v.at[j],
                    send_sem=r_send.at[0],
                    recv_sem=r_recv.at[j],
                    device_id=(s, j),
                    device_id_type=MESH,
                ).wait_recv()
                value = prec_v[j].astype(F32)
                total = value if total is None else total + value
            pan_v[mine] = total.astype(BF16)
            for k in range(1, n):
                spread_copy(k).start()

    def face(f):
        return slice(f * w, (f + 1) * w)

    @pl.when(last)
    def _():
        for b in range(3):
            load_in[b].wait()
            part = slice(b * third, (b + 1) * third)
            for f in range(faces):
                wide_v[part, face(f)] = dot(cin_v[part, face(f)], inv_v[f]).astype(BF16)
        assemble(0)
        assemble(1)
        for f in range(faces):
            full_v[:, face(f)] = dot(local_v[:, face(f)], inv_v[f])
        sum_panel()
        full_v[...] = full_v[...] - dot(arrived_pair(0), wide_v[:pair, :])
        solved = full_v[...] - dot(arrived_pair(1), wide_v[pair:, :])
        for f in range(faces):
            out_v[:, f, :] = solved[:, face(f)]

    @pl.when(jnp.logical_not(last))
    def _():
        load_out.wait()

        @pl.loop(0, panel // 512)
        def _(b):
            cols = pl.ds(pl.multiple_of(b * 512, 512), 512)
            for f in range(faces):
                wide_v[face(f), cols] = dot(inv_v[f], cout_v[face(f), cols]).astype(BF16)

        @pl.when(jnp.logical_not(first))
        def _():
            wait_in()

            @pl.loop(0, panel // 256)
            def _(b):
                @pl.when((b == 2) & (s == 1))
                def _():
                    send_rows()

                cols = pl.ds(pl.multiple_of(b * 256, 256), 256)
                deep_v[:, cols] = dot(cin_v[...], wide_v[:, cols]).astype(BF16)

        assemble(0)
        acc_v[...] = dot(local_v[:, :half_w], wide_v[:half_w, :])
        assemble(1)
        tail = local_v[:, half_w:]

        @pl.when(first)
        def _():
            for h in range(2):
                send_pair(h, acc_v[:, columns(h)] + dot(tail, wide_v[half_w:, columns(h)]))

        @pl.when(jnp.logical_not(first))
        def _():
            acc_v[...] = acc_v[...] + dot(tail, wide_v[half_w:, :])
            sum_panel()
            acc_v[...] = acc_v[...] - dot(arrived_pair(0), deep_v[:pair, :])
            rest = arrived_pair(1)
            for h in range(2):
                send_pair(h, acc_v[:, columns(h)] - dot(rest, deep_v[pair:, columns(h)]))
            whole = jnp.concatenate([pan_v[c] for c in range(pieces)], axis=1)
            full_v[...] = full_v[...] - dot(whole, cin_v[...])

        for f in range(faces):
            out_v[:, f, :] = dot(full_v[:, face(f)].astype(BF16), inv_v[f])

    store_out = pltpu.make_async_copy(out_v, out_ref.at[0], load_sem.at[9])
    store_out.start()

    for q in range(2):
        for k in range(1, n):
            row_copy(k, q).wait_send()

    @pl.when(jnp.logical_not(last))
    def _():
        for c in range(pieces):
            panel_copy(c).wait_send()

    @pl.when(jnp.logical_not(first) & sums)
    def _():
        for k in range(1, n):
            spread_copy(k).wait_send()

    store_out.wait()


def on_device(
    n, layers, face_rhs, res_rows, row_owner, row_slot, inv_blocks, couple_in, couple_out
):
    _, rhs, faces, w = face_rhs.shape
    count = res_rows.shape[0]
    panel, own_w = couple_in.shape[1:]
    pieces, width = OWNERS, panel // OWNERS
    any_ref = pl.BlockSpec(memory_space=pltpu.HBM)
    return pl.pallas_call(
        functools.partial(kernel, n, layers),
        out_shape=jax.ShapeDtypeStruct((1, rhs, faces, w), F32),
        in_specs=[any_ref] * 7,
        out_specs=any_ref,
        scratch_shapes=[
            pltpu.VMEM((1, count), jnp.int32),
            pltpu.VMEM((1, count), jnp.int32),
            pltpu.VMEM((count, w), F32),
            pltpu.VMEM((rhs, faces, w), F32),
            pltpu.VMEM((faces, w, w), BF16),
            pltpu.VMEM((panel, own_w), BF16),
            pltpu.VMEM((own_w, panel), BF16),
            pltpu.VMEM((panel, own_w), BF16),
            pltpu.VMEM((panel, panel), BF16),
            pltpu.VMEM((n, rhs * faces, w), BF16),
            pltpu.VMEM((n, rhs * faces, w), BF16),
            pltpu.VMEM((rhs, own_w), F32),
            pltpu.VMEM((rhs, own_w), BF16),
            pltpu.VMEM((rhs, panel), F32),
            pltpu.VMEM((rhs, faces, w), F32),
            pltpu.VMEM((pieces, rhs, width), BF16),
            pltpu.VMEM((pieces, rhs, width), BF16),
            pltpu.VMEM((n, rhs, width), BF16),
            pltpu.SemaphoreType.DMA((10,)),
            pltpu.SemaphoreType.DMA((n, 2)),
            pltpu.SemaphoreType.DMA((n, 2)),
            pltpu.SemaphoreType.DMA((pieces,)),
            pltpu.SemaphoreType.DMA((n,)),
            pltpu.SemaphoreType.DMA((n,)),
            pltpu.SemaphoreType.DMA((pieces,)),
        ],
        compiler_params=pltpu.CompilerParams(
            collective_id=0, has_side_effects=True, vmem_limit_bytes=63 * 1024 * 1024
        ),
    )(
        row_owner.reshape(1, count),
        row_slot.reshape(1, count),
        res_rows,
        face_rhs,
        inv_blocks,
        couple_in,
        couple_out,
    )


def solution(mesh):
    return jax.shard_map(
        functools.partial(on_device, mesh.shape["layer"], mesh.shape["sweep"]),
        mesh=mesh,
        in_specs=(
            P("sweep", None, "layer", None),
            P(("sweep", "layer"), None),
            P(("sweep", "layer"), None),
            P(("sweep", "layer")),
            P("sweep", "layer", None, None),
            P("sweep", None, "layer"),
            P("sweep", "layer", None),
        ),
        out_specs=P("sweep", None, "layer", None),
        check_vma=False,
    )
```

```python
import functools

import jax
import jax.numpy as jnp
from jax import lax
from jax.experimental import pallas as pl
from jax.experimental.pallas import tpu as pltpu
from jax.sharding import PartitionSpec as P

MESH = pl.DeviceIdType.MESH
F32 = jnp.float32
BF16 = jnp.bfloat16
OWNERS = 4


def dot(a, b):
    return jnp.dot(a, b, preferred_element_type=F32)


def kernel(
    n, layers,
    owner_ref, slot_ref, rows_ref, face_ref, inv_ref, cin_ref, cout_ref,
    out_ref,
    owner_v, slot_v, rows_v, face_v, inv_v, cin_v, cout_v, wide_v, deep_v,
    send_v, recv_v, full_v, local_v, acc_v, pan_v, part_v, prec_v,
    load_sem, a_send, a_recv, r_send, r_recv, g_send, g_recv,
):
    s = lax.axis_index("sweep")
    i = lax.axis_index("layer")
    rhs, faces, w = face_v.shape
    slots = rhs * faces
    panel = cin_v.shape[0]
    own_w = faces * w
    pieces = OWNERS
    width = panel // pieces
    pair = 2 * width
    low = (n - pieces) // 2
    half = faces // 2
    half_rows = half * rhs
    half_w = half * w
    mine = i - low
    others = sorted(range(1, n), key=lambda k: abs(k - n // 2))
    sums = (mine >= 0) & (mine < pieces)
    first, last = s == 0, s == layers - 1

    def load(src, dst, index):
        return pltpu.make_async_copy(src, dst, load_sem.at[index])

    third = panel // 3
    load_owner = load(owner_ref, owner_v, 0)
    load_slot = load(slot_ref, slot_v, 1)
    load_rows = load(rows_ref, rows_v, 2)
    load_face = load(face_ref.at[0], face_v, 3)
    load_inv = load(inv_ref.at[0], inv_v, 4)
    load_out = load(cout_ref.at[0], cout_v, 5)
    load_in = [
        load(cin_ref.at[0, pl.ds(b * third, third)], cin_v.at[pl.ds(b * third, third)], 6 + b)
        for b in range(3)
    ]
    for copy in (load_owner, load_slot, load_rows):
        copy.start()

    barrier = pltpu.get_barrier_semaphore()
    for k in range(1, n):
        pl.semaphore_signal(
            barrier, inc=1, device_id=(s, lax.rem(i + k, n)), device_id_type=MESH
        )

    @pl.when((s > 0) & sums)
    def _():
        for k in range(n):
            pl.semaphore_signal(
                barrier, inc=1, device_id=(s - 1, lax.rem(i + k, n)), device_id_type=MESH
            )

    load_owner.wait()
    load_slot.wait()
    slot = slot_v[...]
    target = owner_v[...] * slots + (slot % faces) * rhs + slot // faces
    load_rows.wait()
    load_inv.start()

    @pl.when(last)
    def _():
        for copy in load_in:
            copy.start()

    @pl.when(jnp.logical_not(last))
    def _():
        load_out.start()

    load_face.start()

    @pl.when(jnp.logical_not(first | last))
    def _():
        for copy in load_in:
            copy.start()

    rows = rows_v[...].astype(BF16)
    group = 4
    for g in range(0, n, group):
        place = lax.broadcasted_iota(jnp.int32, (group * slots, rows.shape[0]), 0) + g * slots
        hot = jnp.where(place == target, 1.0, 0.0).astype(BF16)
        summed = dot(hot, rows).astype(BF16)
        for j in range(group):
            send_v[g + j] = summed[j * slots : (j + 1) * slots]

    heard = (n - 1) + jnp.where(last, 0, pieces)
    pl.semaphore_wait(barrier, heard)

    def row_copy(k, q):
        to = lax.rem(i + k, n)
        part = pl.ds(q * half_rows, half_rows)
        return pltpu.make_async_remote_copy(
            src_ref=send_v.at[to, part],
            dst_ref=recv_v.at[i, part],
            send_sem=a_send.at[k, q],
            recv_sem=a_recv.at[i, q],
            device_id=(s, to),
            device_id_type=MESH,
        )

    def row_arrival(source, q):
        part = pl.ds(q * half_rows, half_rows)
        return pltpu.make_async_remote_copy(
            src_ref=send_v.at[source, part],
            dst_ref=recv_v.at[source, part],
            send_sem=a_send.at[0, q],
            recv_sem=a_recv.at[source, q],
            device_id=(s, source),
            device_id_type=MESH,
        )

    def send_rows():
        for q in range(2):
            for k in others:
                row_copy(k, q).start()

    def panel_copy(c):
        return pltpu.make_async_remote_copy(
            src_ref=part_v.at[c],
            dst_ref=prec_v.at[i],
            send_sem=r_send.at[c],
            recv_sem=r_recv.at[i],
            device_id=(s + 1, low + c),
            device_id_type=MESH,
        )

    def send_panel(c, value):
        part_v[c] = value.astype(BF16)
        panel_copy(c).start()

    def columns(h):
        return slice(h * pair, (h + 1) * pair)

    def send_pair(h, value):
        for a in range(2):
            send_panel(2 * h + a, value[:, a * width : (a + 1) * width])

    def assemble(q):
        for k in range(1, n):
            row_arrival(lax.rem(i + k, n), q).wait_recv()
        for f in range(q * half, (q + 1) * half):
            part = slice(f * rhs, (f + 1) * rhs)
            total = face_v[:, f, :] + send_v[i, part, :].astype(F32)
            for k in range(1, n):
                total = total + recv_v[lax.rem(i + k, n), part, :].astype(F32)
            local = total.astype(BF16)
            cols = slice(f * w, (f + 1) * w)
            full_v[:, cols] = total
            local_v[:, cols] = local

    @pl.when(jnp.logical_not(s == 1))
    def _():
        send_rows()

    load_inv.wait()
    load_face.wait()

    def wait_in():
        for copy in load_in:
            copy.wait()

    def arrive(c):
        @pl.when(mine != c)
        def _():
            pltpu.make_async_remote_copy(
                src_ref=pan_v.at[c],
                dst_ref=pan_v.at[c],
                send_sem=g_send.at[0],
                recv_sem=g_recv.at[c],
                device_id=(s, low + c),
                device_id_type=MESH,
            ).wait_recv()

    def arrived_pair(h):
        for a in range(2):
            arrive(2 * h + a)
        return jnp.concatenate([pan_v[2 * h], pan_v[2 * h + 1]], axis=1)

    def spread_copy(k):
        return pltpu.make_async_remote_copy(
            src_ref=pan_v.at[mine],
            dst_ref=pan_v.at[mine],
            send_sem=g_send.at[k],
            recv_sem=g_recv.at[mine],
            device_id=(s, lax.rem(i + k, n)),
            device_id_type=MESH,
        )

    def sum_panel():
        @pl.when(sums)
        def _():
            total = None
            for j in range(n):
                pltpu.make_async_remote_copy(
                    src_ref=part_v.at[0],
                    dst_ref=prec_v.at[j],
                    send_sem=r_send.at[0],
                    recv_sem=r_recv.at[j],
                    device_id=(s, j),
                    device_id_type=MESH,
                ).wait_recv()
                value = prec_v[j].astype(F32)
                total = value if total is None else total + value
            pan_v[mine] = total.astype(BF16)
            for k in others:
                spread_copy(k).start()

    def face(f):
        return slice(f * w, (f + 1) * w)

    @pl.when(last)
    def _():
        for b in range(3):
            load_in[b].wait()
            part = slice(b * third, (b + 1) * third)
            for f in range(faces):
                wide_v[part, face(f)] = dot(cin_v[part, face(f)], inv_v[f]).astype(BF16)
        assemble(0)
        assemble(1)
        for f in range(faces):
            full_v[:, face(f)] = dot(local_v[:, face(f)], inv_v[f])
        sum_panel()
        full_v[...] = full_v[...] - dot(arrived_pair(0), wide_v[:pair, :])
        solved = full_v[...] - dot(arrived_pair(1), wide_v[pair:, :])
        for f in range(faces):
            out_ref[0, :, f, :] = solved[:, face(f)]

    @pl.when(jnp.logical_not(last))
    def _():
        load_out.wait()

        @pl.loop(0, panel // 512)
        def _(b):
            cols = pl.ds(pl.multiple_of(b * 512, 512), 512)
            for f in range(faces):
                wide_v[face(f), cols] = dot(inv_v[f], cout_v[face(f), cols]).astype(BF16)

        @pl.when(jnp.logical_not(first))
        def _():
            wait_in()

            @pl.loop(0, panel // 256)
            def _(b):
                @pl.when((b == 2) & (s == 1))
                def _():
                    send_rows()

                @pl.when((b == panel // 256 - 1) & (s == 1))
                def _():
                    sum_panel()

                cols = pl.ds(pl.multiple_of(b * 256, 256), 256)
                deep_v[:, cols] = dot(cin_v[...], wide_v[:, cols]).astype(BF16)

        assemble(0)
        acc_v[...] = dot(local_v[:, :half_w], wide_v[:half_w, :])
        assemble(1)
        tail = local_v[:, half_w:]

        @pl.when(first)
        def _():
            for h in range(2):
                send_pair(h, acc_v[:, columns(h)] + dot(tail, wide_v[half_w:, columns(h)]))

        @pl.when(jnp.logical_not(first))
        def _():
            acc_v[...] = acc_v[...] + dot(tail, wide_v[half_w:, :])

            @pl.when(s > 1)
            def _():
                sum_panel()

            acc_v[...] = acc_v[...] - dot(arrived_pair(0), deep_v[:pair, :])
            rest = arrived_pair(1)
            for h in range(2):
                send_pair(h, acc_v[:, columns(h)] - dot(rest, deep_v[pair:, columns(h)]))
            whole = jnp.concatenate([pan_v[c] for c in range(pieces)], axis=1)
            full_v[...] = full_v[...] - dot(whole, cin_v[...])

        for f in range(faces):
            out_ref[0, :, f, :] = dot(full_v[:, face(f)].astype(BF16), inv_v[f])

    for q in range(2):
        for k in range(1, n):
            row_copy(k, q).wait_send()

    @pl.when(jnp.logical_not(last))
    def _():
        for c in range(pieces):
            panel_copy(c).wait_send()

    @pl.when(jnp.logical_not(first) & sums)
    def _():
        for k in range(1, n):
            spread_copy(k).wait_send()


def on_device(
    n, layers, face_rhs, res_rows, row_owner, row_slot, inv_blocks, couple_in, couple_out
):
    _, rhs, faces, w = face_rhs.shape
    count = res_rows.shape[0]
    panel, own_w = couple_in.shape[1:]
    pieces, width = OWNERS, panel // OWNERS
    any_ref = pl.BlockSpec(memory_space=pltpu.HBM)
    return pl.pallas_call(
        functools.partial(kernel, n, layers),
        out_shape=jax.ShapeDtypeStruct((1, rhs, faces, w), F32),
        in_specs=[any_ref] * 7,
        out_specs=pl.BlockSpec(memory_space=pltpu.VMEM),
        scratch_shapes=[
            pltpu.VMEM((1, count), jnp.int32),
            pltpu.VMEM((1, count), jnp.int32),
            pltpu.VMEM((count, w), F32),
            pltpu.VMEM((rhs, faces, w), F32),
            pltpu.VMEM((faces, w, w), BF16),
            pltpu.VMEM((panel, own_w), BF16),
            pltpu.VMEM((own_w, panel), BF16),
            pltpu.VMEM((panel, own_w), BF16),
            pltpu.VMEM((panel, panel), BF16),
            pltpu.VMEM((n, rhs * faces, w), BF16),
            pltpu.VMEM((n, rhs * faces, w), BF16),
            pltpu.VMEM((rhs, own_w), F32),
            pltpu.VMEM((rhs, own_w), BF16),
            pltpu.VMEM((rhs, panel), F32),
            pltpu.VMEM((pieces, rhs, width), BF16),
            pltpu.VMEM((pieces, rhs, width), BF16),
            pltpu.VMEM((n, rhs, width), BF16),
            pltpu.SemaphoreType.DMA((9,)),
            pltpu.SemaphoreType.DMA((n, 2)),
            pltpu.SemaphoreType.DMA((n, 2)),
            pltpu.SemaphoreType.DMA((pieces,)),
            pltpu.SemaphoreType.DMA((n,)),
            pltpu.SemaphoreType.DMA((n,)),
            pltpu.SemaphoreType.DMA((pieces,)),
        ],
        compiler_params=pltpu.CompilerParams(
            collective_id=0, has_side_effects=True, vmem_limit_bytes=50 * 1024 * 1024
        ),
    )(
        *(
            pltpu.with_memory_space_constraint(operand, pltpu.HBM)
            for operand in (
                row_owner.reshape(1, count),
                row_slot.reshape(1, count),
                res_rows,
                face_rhs,
                inv_blocks,
                couple_in,
                couple_out,
            )
        )
    )


def solution(mesh):
    return jax.shard_map(
        functools.partial(on_device, mesh.shape["layer"], mesh.shape["sweep"]),
        mesh=mesh,
        in_specs=(
            P("sweep", None, "layer", None),
            P(("sweep", "layer"), None),
            P(("sweep", "layer"), None),
            P(("sweep", "layer")),
            P("sweep", "layer", None, None),
            P("sweep", None, "layer"),
            P("sweep", "layer", None),
        ),
        out_specs=P("sweep", None, "layer", None),
        check_vma=False,
    )
```

```python
import functools

import jax
import jax.numpy as jnp
from jax import lax
from jax.experimental import pallas as pl
from jax.experimental.pallas import tpu as pltpu
from jax.sharding import PartitionSpec as P

MESH = pl.DeviceIdType.MESH
F32 = jnp.float32
BF16 = jnp.bfloat16
TEAM = 4


def dot(a, b):
    return jnp.dot(a, b, preferred_element_type=F32)


def kernel(
    n, layers,
    owner_ref, slot_ref, rows_ref, face_ref, inv_ref, cin_ref, cout_ref,
    out_ref,
    owner_v, slot_v, rows_v, face_v, inv_v, cin_v, cout_v, wide_v, deep_v,
    send_v, recv_v, full_v, local_v, acc_v, pan_v, part_v, prec_v,
    load_sem, a_send, a_recv, r_send, r_recv, g_send, g_recv,
):
    s = lax.axis_index("sweep")
    i = lax.axis_index("layer")
    rhs, faces, w = face_v.shape
    panel = cin_v.shape[0]
    own_w = faces * w
    pieces = TEAM
    teams = n // TEAM
    width = panel // pieces
    pair = panel // 2
    team, mine = i // TEAM, i % TEAM
    half = faces // 2
    half_rows = half * rhs
    half_w = half * w
    others = sorted(range(1, n), key=lambda k: abs(k - n // 2))
    first, last = s == 0, s == layers - 1

    def load(src, dst, index):
        return pltpu.make_async_copy(src, dst, load_sem.at[index])

    third = panel // 3
    load_owner = load(owner_ref, owner_v, 0)
    load_slot = load(slot_ref, slot_v, 1)
    load_rows = load(rows_ref, rows_v, 2)
    load_face = load(face_ref.at[0], face_v, 3)
    load_inv = load(inv_ref.at[0], inv_v, 4)
    load_out = load(cout_ref.at[0], cout_v, 5)
    load_in = [
        load(cin_ref.at[0, pl.ds(b * third, third)], cin_v.at[pl.ds(b * third, third)], 6 + b)
        for b in range(3)
    ]
    for copy in (load_owner, load_slot, load_rows):
        copy.start()

    barrier = pltpu.get_barrier_semaphore()
    for k in range(1, n):
        pl.semaphore_signal(
            barrier, inc=1, device_id=(s, lax.rem(i + k, n)), device_id_type=MESH
        )

    @pl.when(s > 0)
    def _():
        for k in range(n):
            pl.semaphore_signal(
                barrier, inc=1, device_id=(s - 1, lax.rem(i + k, n)), device_id_type=MESH
            )

    load_owner.wait()
    load_slot.wait()
    slot = slot_v[...]
    slot_face = slot % faces
    target = (
        (slot_face // half) * (n * half_rows)
        + owner_v[...] * half_rows
        + (slot_face % half) * rhs
        + slot // faces
    )
    load_rows.wait()
    load_inv.start()

    @pl.when(last)
    def _():
        for copy in load_in:
            copy.start()

    @pl.when(jnp.logical_not(last))
    def _():
        load_out.start()

    load_face.start()

    @pl.when(jnp.logical_not(first | last))
    def _():
        for copy in load_in:
            copy.start()

    rows = rows_v[...].astype(BF16)
    def sum_rows(q):
        block = min(n, 8) * half_rows
        for g in range(n * half_rows // block):
            base = q * n * half_rows + g * block
            place = lax.broadcasted_iota(jnp.int32, (block, rows.shape[0]), 0) + base
            hot = jnp.where(place == target, 1.0, 0.0).astype(BF16)
            summed = dot(hot, rows).astype(BF16)
            for j in range(block // half_rows):
                send_v[q, g * (block // half_rows) + j] = summed[
                    j * half_rows : (j + 1) * half_rows
                ]

    def row_copy(k, q):
        to = lax.rem(i + k, n)
        return pltpu.make_async_remote_copy(
            src_ref=send_v.at[q, to],
            dst_ref=recv_v.at[q, i],
            send_sem=a_send.at[k, q],
            recv_sem=a_recv.at[i, q],
            device_id=(s, to),
            device_id_type=MESH,
        )

    def row_arrival(source, q):
        return pltpu.make_async_remote_copy(
            src_ref=send_v.at[q, source],
            dst_ref=recv_v.at[q, source],
            send_sem=a_send.at[0, q],
            recv_sem=a_recv.at[source, q],
            device_id=(s, source),
            device_id_type=MESH,
        )

    def send_rows(q):
        for k in others:
            row_copy(k, q).start()

    def panel_copy(c, m):
        to = lax.rem(team + 1 + m, teams) * TEAM + c
        return pltpu.make_async_remote_copy(
            src_ref=part_v.at[c],
            dst_ref=prec_v.at[i],
            send_sem=r_send.at[m, c],
            recv_sem=r_recv.at[i],
            device_id=(s + 1, to),
            device_id_type=MESH,
        )

    def columns(h):
        return slice(h * pair, (h + 1) * pair)

    def send_pair(h, value):
        per = pieces // 2
        for a in range(per):
            part_v[h * per + a] = value[:, a * width : (a + 1) * width].astype(BF16)
        for m in range(teams):
            for a in range(per):
                panel_copy(h * per + a, m).start()

    def assemble(q):
        for k in range(1, n):
            row_arrival(lax.rem(i + k, n), q).wait_recv()
        for f in range(q * half, (q + 1) * half):
            part = slice((f - q * half) * rhs, (f - q * half + 1) * rhs)
            total = face_v[:, f, :] + send_v[q, i, part, :].astype(F32)
            for k in range(1, n):
                total = total + recv_v[q, lax.rem(i + k, n), part, :].astype(F32)
            local = total.astype(BF16)
            cols = slice(f * w, (f + 1) * w)
            full_v[:, cols] = total
            local_v[:, cols] = local

    sum_rows(0)
    heard = (n - 1) + jnp.where(last, 0, n)
    pl.semaphore_wait(barrier, heard)

    @pl.when(jnp.logical_not(s == 1))
    def _():
        send_rows(0)

    sum_rows(1)

    @pl.when(jnp.logical_not(s == 1))
    def _():
        send_rows(1)

    load_inv.wait()
    load_face.wait()

    def wait_in():
        for copy in load_in:
            copy.wait()

    def arrive(c):
        @pl.when(mine != c)
        def _():
            pltpu.make_async_remote_copy(
                src_ref=pan_v.at[c],
                dst_ref=pan_v.at[c],
                send_sem=g_send.at[0],
                recv_sem=g_recv.at[c],
                device_id=(s, team * TEAM + c),
                device_id_type=MESH,
            ).wait_recv()

    def arrived_pair(h):
        chunks = range(h * pieces // 2, (h + 1) * pieces // 2)
        for c in chunks:
            arrive(c)
        return jnp.concatenate([pan_v[c] for c in chunks], axis=1)

    def spread_copy(m):
        return pltpu.make_async_remote_copy(
            src_ref=pan_v.at[mine],
            dst_ref=pan_v.at[mine],
            send_sem=g_send.at[m],
            recv_sem=g_recv.at[mine],
            device_id=(s, team * TEAM + lax.rem(mine + m, TEAM)),
            device_id_type=MESH,
        )

    def sum_panel():
        total = None
        for j in range(n):
            pltpu.make_async_remote_copy(
                src_ref=part_v.at[0],
                dst_ref=prec_v.at[j],
                send_sem=r_send.at[0, 0],
                recv_sem=r_recv.at[j],
                device_id=(s, j),
                device_id_type=MESH,
            ).wait_recv()
        for j in range(n):
            value = prec_v[j].astype(F32)
            total = value if total is None else total + value
        pan_v[mine] = total.astype(BF16)
        for m in range(1, TEAM):
            spread_copy(m).start()

    def face(f):
        return slice(f * w, (f + 1) * w)

    @pl.when(last)
    def _():
        for b in range(3):
            load_in[b].wait()
            part = slice(b * third, (b + 1) * third)
            for f in range(faces):
                wide_v[part, face(f)] = dot(cin_v[part, face(f)], inv_v[f]).astype(BF16)
        assemble(0)
        assemble(1)
        for f in range(faces):
            full_v[:, face(f)] = dot(local_v[:, face(f)], inv_v[f])
        sum_panel()
        full_v[...] = full_v[...] - dot(arrived_pair(0), wide_v[:pair, :])
        solved = full_v[...] - dot(arrived_pair(1), wide_v[pair:, :])
        for f in range(faces):
            out_ref[0, :, f, :] = solved[:, face(f)]

    @pl.when(jnp.logical_not(last))
    def _():
        load_out.wait()

        @pl.loop(0, panel // 512)
        def _(b):
            cols = pl.ds(pl.multiple_of(b * 512, 512), 512)
            for f in range(faces):
                wide_v[face(f), cols] = dot(inv_v[f], cout_v[face(f), cols]).astype(BF16)

        @pl.when(jnp.logical_not(first))
        def _():
            wait_in()

            @pl.loop(0, panel // 256)
            def _(b):
                @pl.when((b == 2) & (s == 1))
                def _():
                    send_rows(0)
                    send_rows(1)

                @pl.when((b == panel // 256 - 1) & (s == 1))
                def _():
                    sum_panel()

                cols = pl.ds(pl.multiple_of(b * 256, 256), 256)
                deep_v[:, cols] = dot(cin_v[...], wide_v[:, cols]).astype(BF16)

        assemble(0)
        acc_v[...] = dot(local_v[:, :half_w], wide_v[:half_w, :])
        assemble(1)
        tail = local_v[:, half_w:]

        @pl.when(first)
        def _():
            for h in range(2):
                send_pair(h, acc_v[:, columns(h)] + dot(tail, wide_v[half_w:, columns(h)]))

        @pl.when(jnp.logical_not(first))
        def _():
            acc_v[...] = acc_v[...] + dot(tail, wide_v[half_w:, :])

            @pl.when(s > 1)
            def _():
                sum_panel()

            acc_v[...] = acc_v[...] - dot(arrived_pair(0), deep_v[:pair, :])
            rest = arrived_pair(1)
            for h in range(2):
                send_pair(h, acc_v[:, columns(h)] - dot(rest, deep_v[pair:, columns(h)]))
            whole = jnp.concatenate([pan_v[c] for c in range(pieces)], axis=1)
            full_v[...] = full_v[...] - dot(whole, cin_v[...])

        for f in range(faces):
            out_ref[0, :, f, :] = dot(full_v[:, face(f)].astype(BF16), inv_v[f])

    for q in range(2):
        for k in range(1, n):
            row_copy(k, q).wait_send()

    @pl.when(jnp.logical_not(last))
    def _():
        for c in range(pieces):
            for m in range(teams):
                panel_copy(c, m).wait_send()

    @pl.when(jnp.logical_not(first))
    def _():
        for m in range(1, TEAM):
            spread_copy(m).wait_send()


def on_device(
    n, layers, face_rhs, res_rows, row_owner, row_slot, inv_blocks, couple_in, couple_out
):
    _, rhs, faces, w = face_rhs.shape
    count = res_rows.shape[0]
    panel, own_w = couple_in.shape[1:]
    pieces, width = TEAM, panel // TEAM
    any_ref = pl.BlockSpec(memory_space=pltpu.HBM)
    return pl.pallas_call(
        functools.partial(kernel, n, layers),
        out_shape=jax.ShapeDtypeStruct((1, rhs, faces, w), F32),
        in_specs=[any_ref] * 7,
        out_specs=pl.BlockSpec(memory_space=pltpu.VMEM),
        scratch_shapes=[
            pltpu.VMEM((1, count), jnp.int32),
            pltpu.VMEM((1, count), jnp.int32),
            pltpu.VMEM((count, w), F32),
            pltpu.VMEM((rhs, faces, w), F32),
            pltpu.VMEM((faces, w, w), BF16),
            pltpu.VMEM((panel, own_w), BF16),
            pltpu.VMEM((own_w, panel), BF16),
            pltpu.VMEM((panel, own_w), BF16),
            pltpu.VMEM((panel, panel), BF16),
            pltpu.VMEM((2, n, rhs * faces // 2, w), BF16),
            pltpu.VMEM((2, n, rhs * faces // 2, w), BF16),
            pltpu.VMEM((rhs, own_w), F32),
            pltpu.VMEM((rhs, own_w), BF16),
            pltpu.VMEM((rhs, panel), F32),
            pltpu.VMEM((pieces, rhs, width), BF16),
            pltpu.VMEM((pieces, rhs, width), BF16),
            pltpu.VMEM((n, rhs, width), BF16),
            pltpu.SemaphoreType.DMA((9,)),
            pltpu.SemaphoreType.DMA((n, 2)),
            pltpu.SemaphoreType.DMA((n, 2)),
            pltpu.SemaphoreType.DMA((n // TEAM, pieces)),
            pltpu.SemaphoreType.DMA((n,)),
            pltpu.SemaphoreType.DMA((TEAM,)),
            pltpu.SemaphoreType.DMA((pieces,)),
        ],
        compiler_params=pltpu.CompilerParams(
            collective_id=0, has_side_effects=True, vmem_limit_bytes=50 * 1024 * 1024
        ),
    )(
        *(
            pltpu.with_memory_space_constraint(operand, pltpu.HBM)
            for operand in (
                row_owner.reshape(1, count),
                row_slot.reshape(1, count),
                res_rows,
                face_rhs,
                inv_blocks,
                couple_in,
                couple_out,
            )
        )
    )


def solution(mesh):
    return jax.shard_map(
        functools.partial(on_device, mesh.shape["layer"], mesh.shape["sweep"]),
        mesh=mesh,
        in_specs=(
            P("sweep", None, "layer", None),
            P(("sweep", "layer"), None),
            P(("sweep", "layer"), None),
            P(("sweep", "layer")),
            P("sweep", "layer", None, None),
            P("sweep", None, "layer"),
            P("sweep", "layer", None),
        ),
        out_specs=P("sweep", None, "layer", None),
        check_vma=False,
    )
```

```python
import functools

import jax
import jax.numpy as jnp
from jax import lax
from jax.experimental import pallas as pl
from jax.experimental.pallas import tpu as pltpu
from jax.sharding import PartitionSpec as P

MESH = pl.DeviceIdType.MESH
F32 = jnp.float32
BF16 = jnp.bfloat16
TEAM = 4


def dot(a, b):
    return jnp.dot(a, b, preferred_element_type=F32)


def kernel(
    n, layers,
    owner_ref, slot_ref, rows_ref, face_ref, inv_ref, cin_ref, cout_ref,
    out_ref,
    owner_v, slot_v, rows_v, face_v, inv_v, cin_v, cout_v, wide_v, deep_v,
    send_v, recv_v, full_v, local_v, acc_v, pan_v, part_v, prec_v, sum_v,
    load_sem, a_send, a_recv, r_send, r_recv, g_send, g_recv,
):
    s = lax.axis_index("sweep")
    i = lax.axis_index("layer")
    rhs, faces, w = face_v.shape
    panel = cin_v.shape[0]
    own_w = faces * w
    pieces = TEAM
    teams = n // TEAM
    width = panel // pieces
    pair = panel // 2
    team, mine = i // TEAM, i % TEAM
    half = faces // 2
    half_rows = half * rhs
    half_w = half * w
    others = sorted(range(1, n), key=lambda k: abs(k - n // 2))
    first, last = s == 0, s == layers - 1

    def load(src, dst, index):
        return pltpu.make_async_copy(src, dst, load_sem.at[index])

    third = panel // 3
    load_owner = load(owner_ref, owner_v, 0)
    load_slot = load(slot_ref, slot_v, 1)
    load_rows = load(rows_ref, rows_v, 2)
    load_face = load(face_ref.at[0], face_v, 3)
    load_inv = load(inv_ref.at[0], inv_v, 4)
    load_out = load(cout_ref.at[0], cout_v, 5)
    load_in = [
        load(cin_ref.at[0, pl.ds(b * third, third)], cin_v.at[pl.ds(b * third, third)], 6 + b)
        for b in range(3)
    ]
    for copy in (load_owner, load_slot, load_rows):
        copy.start()

    barrier = pltpu.get_barrier_semaphore()
    for k in range(1, n):
        pl.semaphore_signal(
            barrier, inc=1, device_id=(s, lax.rem(i + k, n)), device_id_type=MESH
        )

    @pl.when(s > 0)
    def _():
        for c in range(TEAM):
            pl.semaphore_signal(
                barrier, inc=1, device_id=(s - 1, team * TEAM + c), device_id_type=MESH
            )

    load_owner.wait()
    load_slot.wait()
    slot = slot_v[...]
    slot_face = slot % faces
    target = (
        (slot_face // half) * (n * half_rows)
        + owner_v[...] * half_rows
        + (slot_face % half) * rhs
        + slot // faces
    )
    load_rows.wait()
    load_inv.start()

    @pl.when(last)
    def _():
        for copy in load_in:
            copy.start()

    @pl.when(jnp.logical_not(last))
    def _():
        load_out.start()

    load_face.start()

    @pl.when(jnp.logical_not(first | last))
    def _():
        for copy in load_in:
            copy.start()

    rows = rows_v[...].astype(BF16)
    def sum_rows(q):
        block = min(n, 8) * half_rows
        for g in range(n * half_rows // block):
            base = q * n * half_rows + g * block
            place = lax.broadcasted_iota(jnp.int32, (block, rows.shape[0]), 0) + base
            hot = jnp.where(place == target, 1.0, 0.0).astype(BF16)
            summed = dot(hot, rows).astype(BF16)
            for j in range(block // half_rows):
                send_v[q, g * (block // half_rows) + j] = summed[
                    j * half_rows : (j + 1) * half_rows
                ]

    def row_copy(k, q):
        to = lax.rem(i + k, n)
        return pltpu.make_async_remote_copy(
            src_ref=send_v.at[q, to],
            dst_ref=recv_v.at[q, i],
            send_sem=a_send.at[k, q],
            recv_sem=a_recv.at[i, q],
            device_id=(s, to),
            device_id_type=MESH,
        )

    def row_arrival(source, q):
        return pltpu.make_async_remote_copy(
            src_ref=send_v.at[q, source],
            dst_ref=recv_v.at[q, source],
            send_sem=a_send.at[0, q],
            recv_sem=a_recv.at[source, q],
            device_id=(s, source),
            device_id_type=MESH,
        )

    def send_rows(q):
        for k in others:
            row_copy(k, q).start()

    def panel_copy(c, m):
        to = lax.rem(team + 1 + m, teams) * TEAM + c
        return pltpu.make_async_remote_copy(
            src_ref=part_v.at[c],
            dst_ref=prec_v.at[i],
            send_sem=r_send.at[m, c],
            recv_sem=r_recv.at[i],
            device_id=(s, to),
            device_id_type=MESH,
        )

    def each_panel_copy(c, m, act):
        def run():
            copy = panel_copy(c, m)
            copy.start() if act == "start" else copy.wait_send()

        if m < teams - 1:
            run()
        else:

            @pl.when(mine != c)
            def _():
                run()

    def columns(h):
        return slice(h * pair, (h + 1) * pair)

    def send_pair(h, value):
        per = pieces // 2
        for a in range(per):
            part_v[h * per + a] = value[:, a * width : (a + 1) * width].astype(BF16)
        for m in range(teams):
            for a in range(per):
                each_panel_copy(h * per + a, m, "start")

    def assemble(q):
        for k in range(1, n):
            row_arrival(lax.rem(i + k, n), q).wait_recv()
        for f in range(q * half, (q + 1) * half):
            part = slice((f - q * half) * rhs, (f - q * half + 1) * rhs)
            total = face_v[:, f, :] + send_v[q, i, part, :].astype(F32)
            for k in range(1, n):
                total = total + recv_v[q, lax.rem(i + k, n), part, :].astype(F32)
            local = total.astype(BF16)
            cols = slice(f * w, (f + 1) * w)
            full_v[:, cols] = total
            local_v[:, cols] = local

    sum_rows(0)
    heard = (n - 1) + jnp.where(last, 0, TEAM)
    pl.semaphore_wait(barrier, heard)

    @pl.when(jnp.logical_not(s == 1))
    def _():
        send_rows(0)

    sum_rows(1)

    @pl.when(jnp.logical_not(s == 1))
    def _():
        send_rows(1)

    load_inv.wait()
    load_face.wait()

    def wait_in():
        for copy in load_in:
            copy.wait()

    def arrive(c):
        pltpu.make_async_remote_copy(
            src_ref=pan_v.at[c],
            dst_ref=pan_v.at[c],
            send_sem=g_send.at[0],
            recv_sem=g_recv.at[c],
            device_id=(s, lax.rem(i + 1, n)),
            device_id_type=MESH,
        ).wait_recv()

    def arrived_pair(h):
        chunks = range(h * pieces // 2, (h + 1) * pieces // 2)
        for c in chunks:
            arrive(c)
        return jnp.concatenate([pan_v[c] for c in chunks], axis=1)

    def forward_copy(m):
        return pltpu.make_async_remote_copy(
            src_ref=sum_v,
            dst_ref=pan_v.at[mine],
            send_sem=g_send.at[m],
            recv_sem=g_recv.at[mine],
            device_id=(s + 1, team * TEAM + lax.rem(mine + m, TEAM)),
            device_id_type=MESH,
        )

    forward_order = sorted(range(TEAM), key=lambda m: abs(m - TEAM // 2))

    def forward_panel():
        for k in range(1, n):
            j = lax.rem(i + k, n)
            pltpu.make_async_remote_copy(
                src_ref=sum_v,
                dst_ref=prec_v.at[j],
                send_sem=r_send.at[0, 0],
                recv_sem=r_recv.at[j],
                device_id=(s, j),
                device_id_type=MESH,
            ).wait_recv()
        total = part_v[mine].astype(F32)
        for k in range(1, n):
            total = total + prec_v[lax.rem(i + k, n)].astype(F32)
        sum_v[...] = total.astype(BF16)
        for m in forward_order:
            forward_copy(m).start()

    def face(f):
        return slice(f * w, (f + 1) * w)

    @pl.when(last)
    def _():
        for b in range(3):
            load_in[b].wait()
            part = slice(b * third, (b + 1) * third)
            for f in range(faces):
                wide_v[part, face(f)] = dot(cin_v[part, face(f)], inv_v[f]).astype(BF16)
        assemble(0)
        assemble(1)
        for f in range(faces):
            full_v[:, face(f)] = dot(local_v[:, face(f)], inv_v[f])
        full_v[...] = full_v[...] - dot(arrived_pair(0), wide_v[:pair, :])
        solved = full_v[...] - dot(arrived_pair(1), wide_v[pair:, :])
        for f in range(faces):
            out_ref[0, :, f, :] = solved[:, face(f)]

    @pl.when(jnp.logical_not(last))
    def _():
        load_out.wait()

        @pl.loop(0, panel // 512)
        def _(b):
            cols = pl.ds(pl.multiple_of(b * 512, 512), 512)
            for f in range(faces):
                wide_v[face(f), cols] = dot(inv_v[f], cout_v[face(f), cols]).astype(BF16)

        @pl.when(jnp.logical_not(first))
        def _():
            wait_in()

            @pl.loop(0, panel // 256)
            def _(b):
                @pl.when((b == 2) & (s == 1))
                def _():
                    send_rows(0)
                    send_rows(1)

                cols = pl.ds(pl.multiple_of(b * 256, 256), 256)
                deep_v[:, cols] = dot(cin_v[...], wide_v[:, cols]).astype(BF16)

        assemble(0)
        acc_v[...] = dot(local_v[:, :half_w], wide_v[:half_w, :])
        assemble(1)
        tail = local_v[:, half_w:]

        @pl.when(first)
        def _():
            for h in range(2):
                send_pair(h, acc_v[:, columns(h)] + dot(tail, wide_v[half_w:, columns(h)]))
            forward_panel()

        @pl.when(jnp.logical_not(first))
        def _():
            acc_v[...] = acc_v[...] + dot(tail, wide_v[half_w:, :])
            acc_v[...] = acc_v[...] - dot(arrived_pair(0), deep_v[:pair, :])
            rest = arrived_pair(1)
            for h in range(2):
                send_pair(h, acc_v[:, columns(h)] - dot(rest, deep_v[pair:, columns(h)]))
            forward_panel()
            whole = jnp.concatenate([pan_v[c] for c in range(pieces)], axis=1)
            full_v[...] = full_v[...] - dot(whole, cin_v[...])

        for f in range(faces):
            out_ref[0, :, f, :] = dot(full_v[:, face(f)].astype(BF16), inv_v[f])

    for q in range(2):
        for k in range(1, n):
            row_copy(k, q).wait_send()

    @pl.when(jnp.logical_not(last))
    def _():
        for c in range(pieces):
            for m in range(teams):
                each_panel_copy(c, m, "wait_send")
        for m in range(TEAM):
            forward_copy(m).wait_send()


def on_device(
    n, layers, face_rhs, res_rows, row_owner, row_slot, inv_blocks, couple_in, couple_out
):
    _, rhs, faces, w = face_rhs.shape
    count = res_rows.shape[0]
    panel, own_w = couple_in.shape[1:]
    pieces, width = TEAM, panel // TEAM
    any_ref = pl.BlockSpec(memory_space=pltpu.HBM)
    return pl.pallas_call(
        functools.partial(kernel, n, layers),
        out_shape=jax.ShapeDtypeStruct((1, rhs, faces, w), F32),
        in_specs=[any_ref] * 7,
        out_specs=pl.BlockSpec(memory_space=pltpu.VMEM),
        scratch_shapes=[
            pltpu.VMEM((1, count), jnp.int32),
            pltpu.VMEM((1, count), jnp.int32),
            pltpu.VMEM((count, w), F32),
            pltpu.VMEM((rhs, faces, w), F32),
            pltpu.VMEM((faces, w, w), BF16),
            pltpu.VMEM((panel, own_w), BF16),
            pltpu.VMEM((own_w, panel), BF16),
            pltpu.VMEM((panel, own_w), BF16),
            pltpu.VMEM((panel, panel), BF16),
            pltpu.VMEM((2, n, rhs * faces // 2, w), BF16),
            pltpu.VMEM((2, n, rhs * faces // 2, w), BF16),
            pltpu.VMEM((rhs, own_w), F32),
            pltpu.VMEM((rhs, own_w), BF16),
            pltpu.VMEM((rhs, panel), F32),
            pltpu.VMEM((pieces, rhs, width), BF16),
            pltpu.VMEM((pieces, rhs, width), BF16),
            pltpu.VMEM((n, rhs, width), BF16),
            pltpu.VMEM((rhs, width), BF16),
            pltpu.SemaphoreType.DMA((9,)),
            pltpu.SemaphoreType.DMA((n, 2)),
            pltpu.SemaphoreType.DMA((n, 2)),
            pltpu.SemaphoreType.DMA((n // TEAM, pieces)),
            pltpu.SemaphoreType.DMA((n,)),
            pltpu.SemaphoreType.DMA((TEAM,)),
            pltpu.SemaphoreType.DMA((pieces,)),
        ],
        compiler_params=pltpu.CompilerParams(
            collective_id=0, has_side_effects=True, vmem_limit_bytes=50 * 1024 * 1024
        ),
    )(
        *(
            pltpu.with_memory_space_constraint(operand, pltpu.HBM)
            for operand in (
                row_owner.reshape(1, count),
                row_slot.reshape(1, count),
                res_rows,
                face_rhs,
                inv_blocks,
                couple_in,
                couple_out,
            )
        )
    )


def solution(mesh):
    return jax.shard_map(
        functools.partial(on_device, mesh.shape["layer"], mesh.shape["sweep"]),
        mesh=mesh,
        in_specs=(
            P("sweep", None, "layer", None),
            P(("sweep", "layer"), None),
            P(("sweep", "layer"), None),
            P(("sweep", "layer")),
            P("sweep", "layer", None, None),
            P("sweep", None, "layer"),
            P("sweep", "layer", None),
        ),
        out_specs=P("sweep", None, "layer", None),
        check_vma=False,
    )
```
